32 devices in a mesh: group: 2 (over z_hi), shard: 8 (over y, x, core), tensor: 2 (over z_lo).
Axes of the slice: x: 2, y: 2, z: 4 (z_hi: 2, z_lo: 2; z = z_hi * 2 + z_lo), core: 2. Of those that a mesh axis runs over, the one named last changes fastest.
Arguments:
- down_anchor: float32 [8192, 4096], P('shard', 'tensor'), may hold values from -6 to 6
- down_local: float32 [2, 8192, 4096], P('group', 'shard', 'tensor'), may hold values from -6 to 6
- down_moment: float32 [8192, 4096], P(('shard', 'group'), 'tensor'), may hold values from -4 to 4
- norm_anchor: float32 [2, 4096], P(None, ('shard', 'tensor')), may hold values from 0.5 to 1.5
- norm_local: float32 [2, 2, 4096], P('group', None, ('shard', 'tensor')), may hold values from 0.1 to 1.9
- norm_moment: float32 [2, 4096], P('group', ('shard', 'tensor')), may hold values from -4 to 4
- gate_anchor: float32 [8192, 4096], P('tensor', 'shard'), may hold values from -6 to 6
- gate_local: float32 [2, 8192, 4096], P('group', 'tensor', 'shard'), may hold values from -6 to 6
- gate_moment: float32 [8192, 4096], P('tensor', 'shard'), may hold values from -4 to 4
- factor_basis: float32 [64, 4096], P(None, 'shard'), may hold values from -0.09375 to 0.09375
Outputs:
- new_down_anchor: float32 [8192, 4096], P('shard', 'tensor')
- new_down_moment: float32 [8192, 4096], P(('shard', 'group'), 'tensor')
- new_norm_anchor: float32 [2, 4096], P(None, ('shard', 'tensor'))
- new_norm_moment: float32 [2, 4096], P('group', ('shard', 'tensor'))
- new_gate_anchor: float32 [8192, 4096], P('tensor', 'shard')
- new_gate_moment: float32 [8192, 4096], P('tensor', 'shard')
The draws below stay inside these ranges and needn't reach their ends.
All inputs are finite; a program needn't handle non-finite values.
Results may differ from the reference program's by a relative error of at most 0.000096.
Values sent between devices are 32-bit elements; how exact they have to be, the bound alone decides.
No kernel may reach another device: no remote copies, remote signals or barrier semaphores. Data moves between devices by JAX's collectives and lax.ppermute only.
A program may use at most 128 MiB of HBM per device.

```python
import jax
import jax.numpy as jnp
from jax import lax

D = 4096
FF = 8192
RANK = 64
NORMS = 2
G = 2


def block_levels(rng, extent, pieces, low, largest):
    def one(position, parts):
        steps = jax.random.uniform(jax.random.fold_in(jax.random.fold_in(rng, 6), position), (parts,), jnp.float32, low / len(pieces), largest / len(pieces))
        return jnp.repeat(jnp.exp(steps), extent[position] // parts).reshape((-1,) + (1,) * (len(extent) - position - 1))

    loudness = one(*pieces[0])
    for cut in pieces[1:]:
        loudness = loudness * one(*cut)
    return loudness


def normal_values(stream_key, dims, scale, limit, pieces=(), kind=jnp.bfloat16):
    factor_of = block_levels(stream_key, dims, pieces, -0.22, 0.18) if pieces else 1.0
    result = jax.random.normal(stream_key, dims, jnp.float32) * scale * factor_of
    return jnp.minimum(jnp.maximum(result, -limit), limit).astype(kind)


def setup_inputs(seed: int = 0) -> dict:
    keys = jax.random.split(jax.random.key(seed), 11)
    down_anchor = normal_values(keys[0], (FF, D), 1.0, 6.0, ((0, 8), (1, 2)), jnp.float32)
    down_local = normal_values(keys[1], (G, FF, D), 1.0, 6.0, ((0, 2), (1, 8), (2, 2)), jnp.float32)
    down_moment = normal_values(keys[2], (FF, D), 0.5, 4.0, ((0, 16), (1, 2)), jnp.float32)
    norm_anchor = jnp.clip(1.0 + 0.1 * jax.random.normal(keys[3], (NORMS, D), jnp.float32), 0.5, 1.5)
    norm_local = jnp.clip(1.0 + 0.18 * jax.random.normal(keys[4], (G, NORMS, D), jnp.float32), 0.1, 1.9)
    norm_moment = normal_values(keys[5], (NORMS, D), 0.5, 4.0, ((0, 2), (1, 16)), jnp.float32)
    gate_anchor = normal_values(keys[6], (FF, D), 1.0, 6.0, ((0, 2), (1, 8)), jnp.float32)
    gate_local = normal_values(keys[7], (G, FF, D), 1.0, 6.0, ((0, 2), (1, 2), (2, 8)), jnp.float32)
    gate_moment = normal_values(keys[8], (FF, D), 0.5, 4.0, ((0, 2), (1, 8)), jnp.float32)
    factor_basis = normal_values(keys[9], (RANK, D), D ** -0.5, 0.09375, ((1, 8),), jnp.float32)
    return dict(down_anchor=down_anchor, down_local=down_local, down_moment=down_moment, norm_anchor=norm_anchor, norm_local=norm_local, norm_moment=norm_moment, gate_anchor=gate_anchor, gate_local=gate_local, gate_moment=gate_moment, factor_basis=factor_basis)


outer_rate = 0.7
momentum = 0.9


def advance(anchor, moment, delta):
    moment_next = momentum * moment + delta
    anchor_next = anchor - outer_rate * (delta + momentum * moment_next)
    return anchor_next, moment_next


def reference(down_anchor, down_local, down_moment, norm_anchor, norm_local, norm_moment, gate_anchor, gate_local, gate_moment, factor_basis):
    groups = down_local.shape[0]
    down_delta = jnp.sum(down_anchor[None] - down_local, axis=0) / groups
    norm_delta = jnp.sum(norm_anchor[None] - norm_local, axis=0) / groups
    summed = jnp.sum(gate_anchor[None] - gate_local, axis=0)
    factors = jnp.dot(factor_basis, summed.T, precision=lax.Precision.HIGHEST) / groups
    gate_delta = jnp.dot(factors.T, factor_basis, precision=lax.Precision.HIGHEST)
    new_down_anchor, new_down_moment = advance(down_anchor, down_moment, down_delta)
    new_norm_anchor, new_norm_moment = advance(norm_anchor, norm_moment, norm_delta)
    new_gate_anchor, new_gate_moment = advance(gate_anchor, gate_moment, gate_delta)
    return (new_down_anchor, new_down_moment, new_norm_anchor, new_norm_moment, new_gate_anchor, new_gate_moment)
```

```python
import jax
from jax import lax
from jax.sharding import PartitionSpec as P

outer_rate = 0.7
momentum = 0.9
chunks = 8


def advance(anchor, moment, delta):
    moment_next = momentum * moment + delta
    anchor_next = anchor - outer_rate * (delta + momentum * moment_next)
    return (anchor_next, moment_next)


def rebuild(factors, factor_basis):
    return lax.dot_general(
        factors, factor_basis, (((0,), (0,)), ((), ())), precision=lax.Precision.HIGHEST
    )


def rows_of(array, start, size):
    return lax.dynamic_slice_in_dim(array, start, size, 0)


def swap(array):
    return lax.ppermute(array, "group", [(0, 1), (1, 0)])


def exchange(anchor, local, moment, parts):
    a = outer_rate * (1 + momentum)
    b = outer_rate * momentum * momentum
    group_index = lax.axis_index("group")
    half = moment.shape[0]
    size = half // parts
    own = group_index * half
    other = half - own
    own_local = rows_of(local, own, half)
    mixed = (a / 2) * own_local - b * moment
    received = [swap(rows_of(local, other + i * size, size)) for i in range(parts)]
    mixed_received = [swap(mixed[i * size : (i + 1) * size]) for i in range(parts)]
    anchor_next = (1 - a) * anchor + (a / 2) * local
    moment_next = []
    for i, piece in enumerate(received):
        start = own + i * size
        old = moment[i * size : (i + 1) * size]
        moment_next.append(
            momentum * old
            + rows_of(anchor, start, size)
            - 0.5 * (rows_of(local, start, size) + piece)
        )
        value = rows_of(anchor_next, start, size) + ((a / 2) * piece - b * old)
        anchor_next = lax.dynamic_update_slice_in_dim(anchor_next, value, start, 0)
    for i, piece in enumerate(mixed_received):
        start = other + i * size
        value = rows_of(anchor_next, start, size) + piece
        anchor_next = lax.dynamic_update_slice_in_dim(anchor_next, value, start, 0)
    return anchor_next, lax.concatenate(moment_next, 0)


def body(
    down_anchor,
    down_local,
    down_moment,
    norm_anchor,
    norm_local,
    norm_moment,
    gate_anchor,
    gate_local,
    gate_moment,
    factor_basis,
):
    groups = lax.axis_size("group")
    gate_diff = gate_anchor - gate_local[0]
    partial_factors = lax.dot_general(
        factor_basis, gate_diff, (((1,), (1,)), ((), ())), precision=lax.Precision.HIGHEST
    )
    piece = lax.psum_scatter(partial_factors, "shard", scatter_dimension=0, tiled=True)
    piece = (piece + swap(piece)) / groups
    factors = lax.all_gather(piece, "shard", axis=0, tiled=True)
    new_down_anchor, new_down_moment = exchange(down_anchor, down_local[0], down_moment, chunks)
    new_norm_anchor, new_norm_moment = exchange(norm_anchor, norm_local[0], norm_moment, 1)
    gate_delta = rebuild(factors, factor_basis)
    new_gate_anchor, new_gate_moment = advance(gate_anchor, gate_moment, gate_delta)
    return (
        new_down_anchor,
        new_down_moment,
        new_norm_anchor,
        new_norm_moment,
        new_gate_anchor,
        new_gate_moment,
    )


def solution(mesh):
    placed = (
        P("shard", "tensor"),
        P("group", "shard", "tensor"),
        P(("shard", "group"), "tensor"),
        P(None, ("shard", "tensor")),
        P("group", None, ("shard", "tensor")),
        P("group", ("shard", "tensor")),
        P("tensor", "shard"),
        P("group", "tensor", "shard"),
        P("tensor", "shard"),
        P(None, "shard"),
    )
    return jax.shard_map(
        body,
        mesh=mesh,
        in_specs=placed,
        out_specs=(
            P("shard", "tensor"),
            P(("shard", "group"), "tensor"),
            P(None, ("shard", "tensor")),
            P("group", ("shard", "tensor")),
            P("tensor", "shard"),
            P("tensor", "shard"),
        ),
        check_vma=False,
    )
```

```python
import jax
import jax.numpy as jnp
from jax import lax
from jax.sharding import PartitionSpec as P

outer_rate = 0.7
momentum = 0.9
rate = outer_rate * (1 + momentum)
decay = outer_rate * momentum * momentum
first_sizes = (1, 1, 2, 4, 4, 4, 4, 4, 4, 4)
last_sizes = (4, 4, 4, 4, 4, 4, 4, 2, 1, 1)
after_scatter = 8
after_swap = 3
after_gate = 5


def advance(anchor, moment, delta):
    moment_next = momentum * moment + delta
    anchor_next = anchor - outer_rate * (delta + momentum * moment_next)
    return (anchor_next, moment_next)


def rebuild(factors, factor_basis):
    return lax.dot_general(
        factors, factor_basis, (((0,), (0,)), ((), ())), precision=lax.Precision.HIGHEST
    )


def swap(array):
    return lax.ppermute(array, "group", [(0, 1), (1, 0)])


def after(array, *earlier):
    return lax.optimization_barrier((array, *earlier))[0]


def pieces(half, sizes):
    unit = half // sum(sizes)
    start = 0
    for size in sizes:
        yield start * unit, size * unit
        start += size


def exchange_whole(anchor, local, moment):
    group_index = lax.axis_index("group")
    half = moment.shape[0]
    mine = lax.broadcasted_iota(jnp.int32, anchor.shape, 0) // half == group_index
    wide = lax.concatenate([moment, moment], 0)
    mixed = (rate / 2) * local - decay * wide
    received = swap(jnp.where(mine, mixed, local))
    anchor_next = (1 - rate) * anchor + (rate / 2) * local
    anchor_next += jnp.where(mine, (rate / 2) * received - decay * wide, received)
    step = anchor - 0.5 * (local + received)
    moment_next = momentum * moment + lax.dynamic_slice_in_dim(step, group_index * half, half, 0)
    return anchor_next, moment_next


def body(
    down_anchor,
    down_local,
    down_moment,
    norm_anchor,
    norm_local,
    norm_moment,
    gate_anchor,
    gate_local,
    gate_moment,
    factor_basis,
):
    groups = lax.axis_size("group")
    group_index = lax.axis_index("group")
    local = down_local[0]
    half = down_moment.shape[0]
    own = group_index * half
    other = half - own

    def rows_of(array, start, size):
        return lax.dynamic_slice_in_dim(array, start, size, 0)

    spans = list(pieces(half, first_sizes))
    mixed_spans = list(pieces(half, last_sizes))
    sent = [rows_of(local, other + start, size) for start, size in spans]
    mixed = (rate / 2) * rows_of(local, own, half) - decay * down_moment
    mixed_sent = [mixed[start : start + size] for start, size in mixed_spans]

    gate_diff = gate_anchor - gate_local[0]
    partial_factors = lax.dot_general(
        factor_basis, gate_diff, (((1,), (1,)), ((), ())), precision=lax.Precision.HIGHEST
    )
    piece = lax.psum_scatter(partial_factors, "shard", scatter_dimension=0, tiled=True)
    sent[after_scatter] = after(sent[after_scatter], piece)
    piece_other = swap(piece)
    mixed_sent[after_swap] = after(mixed_sent[after_swap], piece_other)
    piece = (piece + piece_other) / groups
    factors = lax.all_gather(piece, "shard", axis=0, tiled=True)
    gate_delta = rebuild(factors, factor_basis)
    new_gate_anchor, new_gate_moment = advance(gate_anchor, gate_moment, gate_delta)
    mixed_sent[after_gate] = after(mixed_sent[after_gate], new_gate_anchor, new_gate_moment)

    received = [swap(part) for part in sent]
    new_norm_anchor, new_norm_moment = exchange_whole(norm_anchor, norm_local[0], norm_moment)
    mixed_received = [swap(part) for part in mixed_sent]

    anchor_next = (1 - rate) * down_anchor + (rate / 2) * local
    moment_next = []
    for (start, size), part in zip(spans, received):
        old = down_moment[start : start + size]
        moment_next.append(
            momentum * old
            + rows_of(down_anchor, own + start, size)
            - 0.5 * (rows_of(local, own + start, size) + part)
        )
        value = rows_of(anchor_next, own + start, size) + ((rate / 2) * part - decay * old)
        anchor_next = lax.dynamic_update_slice_in_dim(anchor_next, value, own + start, 0)
    for (start, size), part in zip(mixed_spans, mixed_received):
        value = rows_of(anchor_next, other + start, size) + part
        anchor_next = lax.dynamic_update_slice_in_dim(anchor_next, value, other + start, 0)
    return (
        anchor_next,
        lax.concatenate(moment_next, 0),
        new_norm_anchor,
        new_norm_moment,
        new_gate_anchor,
        new_gate_moment,
    )


def solution(mesh):
    placed = (
        P("shard", "tensor"),
        P("group", "shard", "tensor"),
        P(("shard", "group"), "tensor"),
        P(None, ("shard", "tensor")),
        P("group", None, ("shard", "tensor")),
        P("group", ("shard", "tensor")),
        P("tensor", "shard"),
        P("group", "tensor", "shard"),
        P("tensor", "shard"),
        P(None, "shard"),
    )
    return jax.shard_map(
        body,
        mesh=mesh,
        in_specs=placed,
        out_specs=(
            P("shard", "tensor"),
            P(("shard", "group"), "tensor"),
            P(None, ("shard", "tensor")),
            P("group", ("shard", "tensor")),
            P("tensor", "shard"),
            P("tensor", "shard"),
        ),
        check_vma=False,
    )
```

```python
import jax
import jax.numpy as jnp
from jax import lax
from jax.sharding import PartitionSpec as P

outer_rate = 0.7
momentum = 0.9
rate = outer_rate * (1 + momentum)
decay = outer_rate * momentum * momentum
first_sizes = (1, 3, 4, 4, 4, 4, 4, 4, 4)
last_sizes = (4, 4, 4, 4, 4, 4, 4, 3, 1)
window = 3
after_scatter = 7
after_swap = 11
after_gate = 14


def advance(anchor, moment, delta):
    moment_next = momentum * moment + delta
    anchor_next = anchor - outer_rate * (delta + momentum * moment_next)
    return (anchor_next, moment_next)


def rebuild(factors, factor_basis):
    return lax.dot_general(
        factors, factor_basis, (((0,), (0,)), ((), ())), precision=lax.Precision.HIGHEST
    )


def swap(array):
    return lax.ppermute(array, "group", [(0, 1), (1, 0)])


def after(array, *earlier):
    return lax.optimization_barrier((array, *earlier))[0]


def pieces(half, sizes):
    unit = half // sum(sizes)
    start = 0
    for size in sizes:
        yield start * unit, size * unit
        start += size


def mine_of(shape, half):
    return lax.broadcasted_iota(jnp.int32, shape, 0) // half == lax.axis_index("group")


def norm_message(local, moment):
    wide = lax.concatenate([moment, moment], 0)
    mixed = (rate / 2) * local - decay * wide
    return jnp.where(mine_of(local.shape, moment.shape[0]), mixed, local)


def norm_finish(anchor, local, moment, received):
    half = moment.shape[0]
    wide = lax.concatenate([moment, moment], 0)
    mine = mine_of(anchor.shape, half)
    anchor_next = (1 - rate) * anchor + (rate / 2) * local
    anchor_next += jnp.where(mine, (rate / 2) * received - decay * wide, received)
    step = anchor - 0.5 * (local + received)
    own = lax.axis_index("group") * half
    return anchor_next, momentum * moment + lax.dynamic_slice_in_dim(step, own, half, 0)


def body(
    down_anchor,
    down_local,
    down_moment,
    norm_anchor,
    norm_local,
    norm_moment,
    gate_anchor,
    gate_local,
    gate_moment,
    factor_basis,
):
    groups = lax.axis_size("group")
    group_index = lax.axis_index("group")
    local = down_local[0]
    half = down_moment.shape[0]
    own = group_index * half
    other = half - own

    def rows_of(array, start, size):
        return lax.dynamic_slice_in_dim(array, start, size, 0)

    spans = list(pieces(half, first_sizes))
    mixed_spans = list(pieces(half, last_sizes))
    mixed = (rate / 2) * rows_of(local, own, half) - decay * down_moment

    gate_diff = gate_anchor - gate_local[0]
    partial_factors = lax.dot_general(
        factor_basis, gate_diff, (((1,), (1,)), ((), ())), precision=lax.Precision.HIGHEST
    )
    piece = lax.psum_scatter(partial_factors, "shard", scatter_dimension=0, tiled=True)
    piece_other = swap(piece)

    parts = []
    cut = local
    for i, (start, size) in enumerate(spans + mixed_spans):
        if i < len(spans):
            part = rows_of(cut, other + start, size)
            if i < window:
                cut = after(local, part)
        else:
            part = mixed[start : start + size]
        ties = [parts[i - window]] if i >= window else []
        if i == after_scatter:
            ties.append(piece)
        if i == after_swap:
            ties.append(piece_sum)
        if i == after_gate:
            ties += [new_gate_anchor, new_gate_moment]
        parts.append(swap(after(part, *ties)))
        if i == 0:
            norm_sent = after(norm_message(norm_local[0], norm_moment), parts[0])
            norm_received = swap(norm_sent)
        if i == after_scatter:
            piece_sum = piece + after(piece_other, parts[i - 1])
            factors = lax.all_gather(piece_sum / groups, "shard", axis=0, tiled=True)
            gate_delta = rebuild(factors, factor_basis)
            new_gate_anchor, new_gate_moment = advance(gate_anchor, gate_moment, gate_delta)
    received, mixed_received = parts[: len(spans)], parts[len(spans) :]
    norm_received = after(norm_received, parts[after_swap])
    new_norm_anchor, new_norm_moment = norm_finish(
        norm_anchor, norm_local[0], norm_moment, norm_received
    )

    anchor_next = (1 - rate) * down_anchor + (rate / 2) * local
    moment_next = []
    for (start, size), part in zip(spans, received):
        old = down_moment[start : start + size]
        moment_next.append(
            momentum * old
            + rows_of(down_anchor, own + start, size)
            - 0.5 * (rows_of(local, own + start, size) + part)
        )
        value = rows_of(anchor_next, own + start, size) + ((rate / 2) * part - decay * old)
        anchor_next = lax.dynamic_update_slice_in_dim(anchor_next, value, own + start, 0)
    for (start, size), part in zip(mixed_spans, mixed_received):
        value = rows_of(anchor_next, other + start, size) + part
        anchor_next = lax.dynamic_update_slice_in_dim(anchor_next, value, other + start, 0)
    return (
        anchor_next,
        lax.concatenate(moment_next, 0),
        new_norm_anchor,
        new_norm_moment,
        new_gate_anchor,
        new_gate_moment,
    )


def solution(mesh):
    placed = (
        P("shard", "tensor"),
        P("group", "shard", "tensor"),
        P(("shard", "group"), "tensor"),
        P(None, ("shard", "tensor")),
        P("group", None, ("shard", "tensor")),
        P("group", ("shard", "tensor")),
        P("tensor", "shard"),
        P("group", "tensor", "shard"),
        P("tensor", "shard"),
        P(None, "shard"),
    )
    return jax.shard_map(
        body,
        mesh=mesh,
        in_specs=placed,
        out_specs=(
            P("shard", "tensor"),
            P(("shard", "group"), "tensor"),
            P(None, ("shard", "tensor")),
            P("group", ("shard", "tensor")),
            P("tensor", "shard"),
            P("tensor", "shard"),
        ),
        check_vma=False,
    )
```

```python
import jax
import jax.numpy as jnp
from jax import lax
from jax.sharding import PartitionSpec as P

outer_rate = 0.7
momentum = 0.9
rate = outer_rate * (1 + momentum)
decay = outer_rate * momentum * momentum
first_sizes = (1, 3, 4) + (2,) * 12
last_sizes = (2,) * 14 + (3, 1)
window = 3
chain_start = 2
chain_end = 23


def advance(anchor, moment, delta):
    moment_next = momentum * moment + delta
    anchor_next = anchor - outer_rate * (delta + momentum * moment_next)
    return (anchor_next, moment_next)


def rebuild(factors, factor_basis):
    return lax.dot_general(
        factors, factor_basis, (((0,), (0,)), ((), ())), precision=lax.Precision.HIGHEST
    )


def swap(array):
    return lax.ppermute(array, "group", [(0, 1), (1, 0)])


def across(array, k):
    shards = lax.axis_size("shard")
    return lax.ppermute(array, "shard", [(i, i ^ k) for i in range(shards)])


def after(array, *earlier):
    return lax.optimization_barrier((array, *earlier))[0]


def pieces(half, sizes):
    unit = half // sum(sizes)
    start = 0
    for size in sizes:
        yield start * unit, size * unit
        start += size


def factor_chain(value, bits):
    for bit in bits:
        rest = value.shape[0] // 2
        received = yield value[rest:], across(value[rest:], bit)
        value = value[:rest] + received
    received = yield value, swap(value)
    value = (value + received) / lax.axis_size("group")
    for bit in reversed(bits):
        received = yield value, across(value, bit)
        value = lax.concatenate([value, received], 0)
    return value


def mine_of(shape, half):
    return lax.broadcasted_iota(jnp.int32, shape, 0) // half == lax.axis_index("group")


def norm_message(local, moment):
    wide = lax.concatenate([moment, moment], 0)
    mixed = (rate / 2) * local - decay * wide
    return jnp.where(mine_of(local.shape, moment.shape[0]), mixed, local)


def norm_finish(anchor, local, moment, received):
    half = moment.shape[0]
    wide = lax.concatenate([moment, moment], 0)
    mine = mine_of(anchor.shape, half)
    anchor_next = (1 - rate) * anchor + (rate / 2) * local
    anchor_next += jnp.where(mine, (rate / 2) * received - decay * wide, received)
    step = anchor - 0.5 * (local + received)
    own = lax.axis_index("group") * half
    return anchor_next, momentum * moment + lax.dynamic_slice_in_dim(step, own, half, 0)


def body(
    down_anchor,
    down_local,
    down_moment,
    norm_anchor,
    norm_local,
    norm_moment,
    gate_anchor,
    gate_local,
    gate_moment,
    factor_basis,
):
    groups = lax.axis_size("group")
    group_index = lax.axis_index("group")
    local = down_local[0]
    half = down_moment.shape[0]
    own = group_index * half
    other = half - own

    def rows_of(array, start, size):
        return lax.dynamic_slice_in_dim(array, start, size, 0)

    spans = list(pieces(half, first_sizes))
    mixed_spans = list(pieces(half, last_sizes))
    mixed = (rate / 2) * rows_of(local, own, half) - decay * down_moment

    shards = lax.axis_size("shard")
    bits = [1 << n for n in range(shards.bit_length() - 1)]
    masks = [0]
    for bit in reversed(bits):
        masks += [mask | bit for mask in masks]
    block = factor_basis.shape[0] // shards
    basis = lax.concatenate(
        [rows_of(factor_basis, (lax.axis_index("shard") ^ mask) * block, block) for mask in masks],
        0,
    )
    gate_diff = gate_anchor - gate_local[0]
    partial_factors = lax.dot_general(
        basis, gate_diff, (((1,), (1,)), ((), ())), precision=lax.Precision.HIGHEST
    )
    chain = factor_chain(partial_factors, bits)

    stride = (chain_end - chain_start) // (2 * len(bits) + 1)
    parts = []
    cut = local
    step_at = chain_start
    step_sent = step_received = gate = None
    for i, (start, size) in enumerate(spans + mixed_spans):
        if i < len(spans):
            part = rows_of(cut, other + start, size)
            if i < window:
                cut = after(local, part)
        else:
            part = mixed[start : start + size]
        ties = [parts[i - window]] if i >= window else []
        if step_sent is not None:
            ties.append(step_sent)
            step_sent = None
        if gate is not None and i == step_at + window:
            ties += gate
        parts.append(swap(after(part, *ties)))
        if i == 0:
            norm_sent = after(norm_message(norm_local[0], norm_moment), parts[0])
            norm_received = swap(norm_sent)
        if gate is None and i == step_at:
            if step_received is not None:
                step_received = after(step_received, parts[i - stride])
            try:
                step_sent, step_received = chain.send(step_received)
                step_at += stride
            except StopIteration as end:
                gate = advance(gate_anchor, gate_moment, rebuild(end.value, basis))
    new_gate_anchor, new_gate_moment = gate
    received, mixed_received = parts[: len(spans)], parts[len(spans) :]
    norm_received = after(norm_received, parts[chain_end])
    new_norm_anchor, new_norm_moment = norm_finish(
        norm_anchor, norm_local[0], norm_moment, norm_received
    )

    anchor_next = (1 - rate) * down_anchor + (rate / 2) * local
    moment_next = []
    for (start, size), part in zip(spans, received):
        old = down_moment[start : start + size]
        moment_next.append(
            momentum * old
            + rows_of(down_anchor, own + start, size)
            - 0.5 * (rows_of(local, own + start, size) + part)
        )
        value = rows_of(anchor_next, own + start, size) + ((rate / 2) * part - decay * old)
        anchor_next = lax.dynamic_update_slice_in_dim(anchor_next, value, own + start, 0)
    for (start, size), part in zip(mixed_spans, mixed_received):
        value = rows_of(anchor_next, other + start, size) + part
        anchor_next = lax.dynamic_update_slice_in_dim(anchor_next, value, other + start, 0)
    return (
        anchor_next,
        lax.concatenate(moment_next, 0),
        new_norm_anchor,
        new_norm_moment,
        new_gate_anchor,
        new_gate_moment,
    )


def solution(mesh):
    placed = (
        P("shard", "tensor"),
        P("group", "shard", "tensor"),
        P(("shard", "group"), "tensor"),
        P(None, ("shard", "tensor")),
        P("group", None, ("shard", "tensor")),
        P("group", ("shard", "tensor")),
        P("tensor", "shard"),
        P("group", "tensor", "shard"),
        P("tensor", "shard"),
        P(None, "shard"),
    )
    return jax.shard_map(
        body,
        mesh=mesh,
        in_specs=placed,
        out_specs=(
            P("shard", "tensor"),
            P(("shard", "group"), "tensor"),
            P(None, ("shard", "tensor")),
            P("group", ("shard", "tensor")),
            P("tensor", "shard"),
            P("tensor", "shard"),
        ),
        check_vma=False,
    )
```

```python
import jax
import jax.numpy as jnp
from jax import lax
from jax.sharding import PartitionSpec as P

outer_rate = 0.7
momentum = 0.9
rate = outer_rate * (1 + momentum)
decay = outer_rate * momentum * momentum
first_sizes = (1, 3, 4) + (2,) * 12
last_sizes = (2,) * 14 + (1, 1, 1, 1)
window = 3
chain_start = 2
chain_end = 23


def advance(anchor, moment, delta):
    moment_next = momentum * moment + delta
    anchor_next = anchor - outer_rate * (delta + momentum * moment_next)
    return (anchor_next, moment_next)


def rebuild(factors, factor_basis):
    return lax.dot_general(
        factors, factor_basis, (((0,), (0,)), ((), ())), precision=lax.Precision.HIGHEST
    )


def swap(array):
    return lax.ppermute(array, "group", [(0, 1), (1, 0)])


def across(array, k):
    shards = lax.axis_size("shard")
    return lax.ppermute(array, "shard", [(i, i ^ k) for i in range(shards)])


def after(array, *earlier):
    return lax.optimization_barrier((array, *earlier))[0]


def pieces(half, sizes):
    unit = half // sum(sizes)
    start = 0
    for size in sizes:
        yield start * unit, size * unit
        start += size


def factor_chain(value, bits):
    for bit in bits:
        rest = value.shape[0] // 2
        received = yield value[rest:], across(value[rest:], bit)
        value = value[:rest] + received
    received = yield value, swap(value)
    value = (value + received) / lax.axis_size("group")
    for bit in reversed(bits):
        received = yield value, across(value, bit)
        value = lax.concatenate([value, received], 0)
    return value


def mine_of(shape, half):
    return lax.broadcasted_iota(jnp.int32, shape, 0) // half == lax.axis_index("group")


def norm_message(local, moment):
    wide = lax.concatenate([moment, moment], 0)
    mixed = (rate / 2) * local - decay * wide
    return jnp.where(mine_of(local.shape, moment.shape[0]), mixed, local)


def norm_finish(anchor, local, moment, received):
    half = moment.shape[0]
    wide = lax.concatenate([moment, moment], 0)
    mine = mine_of(anchor.shape, half)
    anchor_next = (1 - rate) * anchor + (rate / 2) * local
    anchor_next += jnp.where(mine, (rate / 2) * received - decay * wide, received)
    step = anchor - 0.5 * (local + received)
    own = lax.axis_index("group") * half
    return anchor_next, momentum * moment + lax.dynamic_slice_in_dim(step, own, half, 0)


def body(
    down_anchor,
    down_local,
    down_moment,
    norm_anchor,
    norm_local,
    norm_moment,
    gate_anchor,
    gate_local,
    gate_moment,
    factor_basis,
):
    groups = lax.axis_size("group")
    group_index = lax.axis_index("group")
    local = down_local[0]
    half = down_moment.shape[0]
    own = group_index * half
    other = half - own

    def rows_of(array, start, size):
        return lax.dynamic_slice_in_dim(array, start, size, 0)

    spans = list(pieces(half, first_sizes))
    mixed_spans = list(pieces(half, last_sizes))

    shards = lax.axis_size("shard")
    bits = [1 << n for n in range(shards.bit_length() - 1)]
    masks = [0]
    for bit in reversed(bits):
        masks += [mask | bit for mask in masks]
    block = factor_basis.shape[0] // shards
    basis = lax.concatenate(
        [rows_of(factor_basis, (lax.axis_index("shard") ^ mask) * block, block) for mask in masks],
        0,
    )
    gate_diff = gate_anchor - gate_local[0]
    partial_factors = lax.dot_general(
        basis, gate_diff, (((1,), (1,)), ((), ())), precision=lax.Precision.HIGHEST
    )
    chain = factor_chain(partial_factors, bits)

    stride = (chain_end - chain_start) // (2 * len(bits) + 1)
    parts = []
    cut = local
    step_at = chain_start
    step_sent = step_received = gate = None
    for i, (start, size) in enumerate(spans + mixed_spans):
        if i < len(spans):
            part = rows_of(cut, other + start, size)
            if i < window:
                cut = after(local, part)
        else:
            part = mixed[start : start + size]
        ties = [parts[i - window]] if i >= window else []
        if step_sent is not None:
            ties.append(step_sent)
            step_sent = None
        if gate is not None and i == step_at + window:
            ties += gate
        parts.append(swap(after(part, *ties)))
        if i == 1:
            mixed = (rate / 2) * rows_of(local, own, half) - decay * after(down_moment, parts[1])
            anchor_next = (1 - rate) * after(down_anchor, parts[1]) + (rate / 2) * local
        if i == 0:
            norm_sent = after(norm_message(norm_local[0], norm_moment), parts[0])
            norm_received = swap(norm_sent)
        if gate is None and i == step_at:
            if step_received is not None:
                step_received = after(step_received, parts[i - stride])
            try:
                step_sent, step_received = chain.send(step_received)
                step_at += stride
            except StopIteration as end:
                gate = advance(gate_anchor, gate_moment, rebuild(end.value, basis))
    new_gate_anchor, new_gate_moment = gate
    received, mixed_received = parts[: len(spans)], parts[len(spans) :]
    norm_received = after(norm_received, parts[chain_end])
    new_norm_anchor, new_norm_moment = norm_finish(
        norm_anchor, norm_local[0], norm_moment, norm_received
    )

    moment_next = []
    for (start, size), part in zip(spans, received):
        old = down_moment[start : start + size]
        moment_next.append(
            momentum * old
            + rows_of(down_anchor, own + start, size)
            - 0.5 * (rows_of(local, own + start, size) + part)
        )
        value = rows_of(anchor_next, own + start, size) + ((rate / 2) * part - decay * old)
        anchor_next = lax.dynamic_update_slice_in_dim(anchor_next, value, own + start, 0)
    for (start, size), part in zip(mixed_spans, mixed_received):
        value = rows_of(anchor_next, other + start, size) + part
        anchor_next = lax.dynamic_update_slice_in_dim(anchor_next, value, other + start, 0)
    return (
        anchor_next,
        lax.concatenate(moment_next, 0),
        new_norm_anchor,
        new_norm_moment,
        new_gate_anchor,
        new_gate_moment,
    )


def solution(mesh):
    placed = (
        P("shard", "tensor"),
        P("group", "shard", "tensor"),
        P(("shard", "group"), "tensor"),
        P(None, ("shard", "tensor")),
        P("group", None, ("shard", "tensor")),
        P("group", ("shard", "tensor")),
        P("tensor", "shard"),
        P("group", "tensor", "shard"),
        P("tensor", "shard"),
        P(None, "shard"),
    )
    return jax.shard_map(
        body,
        mesh=mesh,
        in_specs=placed,
        out_specs=(
            P("shard", "tensor"),
            P(("shard", "group"), "tensor"),
            P(None, ("shard", "tensor")),
            P("group", ("shard", "tensor")),
            P("tensor", "shard"),
            P("tensor", "shard"),
        ),
        check_vma=False,
    )
```

```python
import functools

import jax
import jax.numpy as jnp
from jax import lax
from jax.experimental import pallas as pl
from jax.experimental.pallas import tpu as pltpu
from jax.sharding import PartitionSpec as P

outer_rate = 0.7
momentum = 0.9
rate = outer_rate * (1 + momentum)
decay = outer_rate * momentum * momentum
first_sizes = (1, 3, 6, 6)
last_sizes = (4, 4, 2, 2, 2, 1, 1)
window = 3
gate_before = 8


def advance(anchor, moment, delta):
    moment_next = momentum * moment + delta
    anchor_next = anchor - outer_rate * (delta + momentum * moment_next)
    return (anchor_next, moment_next)


def rebuild(factors, factor_basis):
    return lax.dot_general(
        factors, factor_basis, (((0,), (0,)), ((), ())), precision=lax.Precision.HIGHEST
    )


def swap(array):
    return lax.ppermute(array, "group", [(0, 1), (1, 0)])


def across(array, k):
    shards = lax.axis_size("shard")
    return lax.ppermute(array, "shard", [(i, i ^ k) for i in range(shards)])


def after(array, *earlier):
    return lax.optimization_barrier((array, *earlier))[0]


def pieces(half, sizes):
    unit = half // sum(sizes)
    start = 0
    for size in sizes:
        yield start * unit, size * unit
        start += size


def add_kernel(start, half, part, _, total, rows, sem):
    other = (1 - lax.axis_index("group")) * half
    span = total.at[pl.ds(pl.multiple_of(other + start, 8), part.shape[0])]
    read = pltpu.make_async_copy(span, rows, sem)
    read.start()
    read.wait()
    rows[...] += part[...]
    write = pltpu.make_async_copy(rows, span, sem)
    write.start()
    write.wait()


def add_rows(total, part, start, half):
    return pl.pallas_call(
        functools.partial(add_kernel, start, half),
        out_shape=jax.ShapeDtypeStruct(total.shape, total.dtype),
        in_specs=[
            pl.BlockSpec(memory_space=pltpu.VMEM),
            pl.BlockSpec(memory_space=pltpu.HBM),
        ],
        out_specs=pl.BlockSpec(memory_space=pltpu.HBM),
        scratch_shapes=[pltpu.VMEM(part.shape, part.dtype), pltpu.SemaphoreType.DMA],
        input_output_aliases={1: 0},
        cost_estimate=pl.CostEstimate(
            flops=part.size, bytes_accessed=12 * part.size, transcendentals=0
        ),
    )(part, total)


def sum_factors(value, bits):
    for bit in bits:
        rest = value.shape[0] // 2
        value = value[:rest] + across(value[rest:], bit)
    value = (value + swap(value)) / lax.axis_size("group")
    for bit in reversed(bits):
        value = lax.concatenate([value, across(value, bit)], 0)
    return value


def mine_of(shape, half):
    return lax.broadcasted_iota(jnp.int32, shape, 0) // half == lax.axis_index("group")


def norm_message(local, moment):
    wide = lax.concatenate([moment, moment], 0)
    mixed = (rate / 2) * local - decay * wide
    return jnp.where(mine_of(local.shape, moment.shape[0]), mixed, local)


def norm_finish(anchor, local, moment, received):
    half = moment.shape[0]
    wide = lax.concatenate([moment, moment], 0)
    mine = mine_of(anchor.shape, half)
    anchor_next = (1 - rate) * anchor + (rate / 2) * local
    anchor_next += jnp.where(mine, (rate / 2) * received - decay * wide, received)
    step = anchor - 0.5 * (local + received)
    own = lax.axis_index("group") * half
    return anchor_next, momentum * moment + lax.dynamic_slice_in_dim(step, own, half, 0)


def body(
    down_anchor,
    down_local,
    down_moment,
    norm_anchor,
    norm_local,
    norm_moment,
    gate_anchor,
    gate_local,
    gate_moment,
    factor_basis,
):
    groups = lax.axis_size("group")
    group_index = lax.axis_index("group")
    local = down_local[0]
    half = down_moment.shape[0]
    own = group_index * half
    other = half - own

    def rows_of(array, start, size):
        return lax.dynamic_slice_in_dim(array, start, size, 0)

    spans = list(pieces(half, first_sizes))
    mixed_spans = list(pieces(half, last_sizes))

    shards = lax.axis_size("shard")
    bits = [1 << n for n in range(shards.bit_length() - 1)]
    masks = [0]
    for bit in reversed(bits):
        masks += [mask | bit for mask in masks]
    block = factor_basis.shape[0] // shards
    basis = lax.concatenate(
        [rows_of(factor_basis, (lax.axis_index("shard") ^ mask) * block, block) for mask in masks],
        0,
    )
    gate_diff = gate_anchor - gate_local[0]
    partial_factors = lax.dot_general(
        basis, gate_diff, (((1,), (1,)), ((), ())), precision=lax.Precision.HIGHEST
    )
    factors = sum_factors(partial_factors, bits)
    gate = advance(gate_anchor, gate_moment, rebuild(factors, basis))
    new_gate_anchor, new_gate_moment = gate

    parts = []
    cut = local
    for i, (start, size) in enumerate(spans + mixed_spans):
        if i < len(spans):
            part = rows_of(cut, other + start, size)
            if i < window:
                cut = after(local, part)
        else:
            part = mixed[start : start + size]
        ties = [parts[i - window]] if i >= window else []
        if i == gate_before:
            ties += gate
        parts.append(swap(after(part, *ties)))
        if i == 0:
            mixed = (rate / 2) * rows_of(local, own, half) - decay * after(down_moment, parts[0])
            anchor_next = (1 - rate) * after(down_anchor, parts[0]) + (rate / 2) * local
            norm_sent = after(norm_message(norm_local[0], norm_moment), parts[0])
            norm_received = swap(norm_sent)
    received, mixed_received = parts[: len(spans)], parts[len(spans) :]
    norm_received = after(norm_received, parts[1])
    new_norm_anchor, new_norm_moment = norm_finish(
        norm_anchor, norm_local[0], norm_moment, norm_received
    )

    moment_next = []
    for (start, size), part in zip(spans, received):
        old = down_moment[start : start + size]
        moment_next.append(
            momentum * old
            + rows_of(down_anchor, own + start, size)
            - 0.5 * (rows_of(local, own + start, size) + part)
        )
        value = rows_of(anchor_next, own + start, size) + ((rate / 2) * part - decay * old)
        anchor_next = lax.dynamic_update_slice_in_dim(anchor_next, value, own + start, 0)
    for (start, size), part in zip(mixed_spans, mixed_received):
        anchor_next = add_rows(anchor_next, part, start, half)
    return (
        anchor_next,
        lax.concatenate(moment_next, 0),
        new_norm_anchor,
        new_norm_moment,
        new_gate_anchor,
        new_gate_moment,
    )


def solution(mesh):
    placed = (
        P("shard", "tensor"),
        P("group", "shard", "tensor"),
        P(("shard", "group"), "tensor"),
        P(None, ("shard", "tensor")),
        P("group", None, ("shard", "tensor")),
        P("group", ("shard", "tensor")),
        P("tensor", "shard"),
        P("group", "tensor", "shard"),
        P("tensor", "shard"),
        P(None, "shard"),
    )
    return jax.shard_map(
        body,
        mesh=mesh,
        in_specs=placed,
        out_specs=(
            P("shard", "tensor"),
            P(("shard", "group"), "tensor"),
            P(None, ("shard", "tensor")),
            P("group", ("shard", "tensor")),
            P("tensor", "shard"),
            P("tensor", "shard"),
        ),
        check_vma=False,
    )
```

```python
import functools

import jax
import jax.numpy as jnp
from jax import lax
from jax.experimental import pallas as pl
from jax.experimental.pallas import tpu as pltpu
from jax.sharding import PartitionSpec as P

outer_rate = 0.7
momentum = 0.9
rate = outer_rate * (1 + momentum)
decay = outer_rate * momentum * momentum
first_sizes = (1, 7, 12, 12)
last_sizes = (8, 8, 4, 4, 4, 2, 2)
window = 3
gate_before = 6
pinned = 4


def advance(anchor, moment, delta):
    moment_next = momentum * moment + delta
    anchor_next = anchor - outer_rate * (delta + momentum * moment_next)
    return (anchor_next, moment_next)


def rebuild(factors, factor_basis):
    return lax.dot_general(
        factors, factor_basis, (((0,), (0,)), ((), ())), precision=lax.Precision.HIGHEST
    )


def swap(array):
    return lax.ppermute(array, "group", [(0, 1), (1, 0)])


def across(array, k):
    shards = lax.axis_size("shard")
    return lax.ppermute(array, "shard", [(i, i ^ k) for i in range(shards)])


def after(array, *earlier):
    return lax.optimization_barrier((array, *earlier))[0]


def pieces(half, sizes):
    unit = half // sum(sizes)
    start = 0
    for size in sizes:
        yield start * unit, size * unit
        start += size


def add_kernel(start, half, part, _, total, rows, sem):
    other = (1 - lax.axis_index("group")) * half
    span = total.at[pl.ds(pl.multiple_of(other + start, 8), part.shape[0])]
    read = pltpu.make_async_copy(span, rows, sem)
    read.start()
    read.wait()
    rows[...] += part[...]
    write = pltpu.make_async_copy(rows, span, sem)
    write.start()
    write.wait()


def add_rows(total, part, start, half):
    return pl.pallas_call(
        functools.partial(add_kernel, start, half),
        out_shape=jax.ShapeDtypeStruct(total.shape, total.dtype),
        in_specs=[
            pl.BlockSpec(memory_space=pltpu.VMEM),
            pl.BlockSpec(memory_space=pltpu.HBM),
        ],
        out_specs=pl.BlockSpec(memory_space=pltpu.HBM),
        scratch_shapes=[pltpu.VMEM(part.shape, part.dtype), pltpu.SemaphoreType.DMA],
        input_output_aliases={1: 0},
        cost_estimate=pl.CostEstimate(
            flops=part.size, bytes_accessed=12 * part.size, transcendentals=0
        ),
    )(part, total)


def scatter_factors(value, bits):
    for bit in bits:
        rest = value.shape[0] // 2
        value = value[:rest] + across(value[rest:], bit)
    return value


def gather_factors(value, bits):
    for bit in reversed(bits):
        value = lax.concatenate([value, across(value, bit)], 0)
    return value


def mine_of(shape, half):
    return lax.broadcasted_iota(jnp.int32, shape, 0) // half == lax.axis_index("group")


def norm_message(local, moment):
    wide = lax.concatenate([moment, moment], 0)
    mixed = (rate / 2) * local - decay * wide
    return jnp.where(mine_of(local.shape, moment.shape[0]), mixed, local)


def norm_finish(anchor, local, moment, received):
    half = moment.shape[0]
    wide = lax.concatenate([moment, moment], 0)
    mine = mine_of(anchor.shape, half)
    anchor_next = (1 - rate) * anchor + (rate / 2) * local
    anchor_next += jnp.where(mine, (rate / 2) * received - decay * wide, received)
    step = anchor - 0.5 * (local + received)
    own = lax.axis_index("group") * half
    return anchor_next, momentum * moment + lax.dynamic_slice_in_dim(step, own, half, 0)


def body(
    down_anchor,
    down_local,
    down_moment,
    norm_anchor,
    norm_local,
    norm_moment,
    gate_anchor,
    gate_local,
    gate_moment,
    factor_basis,
):
    groups = lax.axis_size("group")
    group_index = lax.axis_index("group")
    local = down_local[0]
    half = down_moment.shape[0]
    own = group_index * half
    other = half - own

    def rows_of(array, start, size):
        return lax.dynamic_slice_in_dim(array, start, size, 0)

    spans = list(pieces(half, first_sizes))
    mixed_spans = list(pieces(half, last_sizes))

    shards = lax.axis_size("shard")
    bits = [1 << n for n in range(shards.bit_length() - 1)]
    masks = [0]
    for bit in reversed(bits):
        masks += [mask | bit for mask in masks]
    block = factor_basis.shape[0] // shards
    basis = lax.concatenate(
        [rows_of(factor_basis, (lax.axis_index("shard") ^ mask) * block, block) for mask in masks],
        0,
    )
    gate_diff = gate_anchor - gate_local[0]
    partial_factors = lax.dot_general(
        basis, gate_diff, (((1,), (1,)), ((), ())), precision=lax.Precision.HIGHEST
    )
    factor_piece = scatter_factors(partial_factors, bits)
    factor_other = swap(factor_piece)

    parts = []
    cut = local
    for i, (start, size) in enumerate(spans + mixed_spans):
        if i < len(spans):
            part = rows_of(cut, other + start, size)
            if i < window:
                cut = after(local, part)
        else:
            part = mixed[start : start + size]
        ties = [parts[i - window]] if i >= window else []
        if i == gate_before:
            ties += gate
        parts.append(swap(after(part, *ties)))
        if i == 0:
            mixed = (rate / 2) * rows_of(local, own, half) - decay * after(down_moment, parts[0])
            anchor_next = (1 - rate) * after(down_anchor, parts[0]) + (rate / 2) * local
            norm_sent = after(norm_message(norm_local[0], norm_moment), parts[0])
            norm_received = swap(norm_sent)
        if i == len(spans) - 1:
            norm_received = after(norm_received, parts[i])
            factor_piece = (factor_piece + after(factor_other, parts[i])) / groups
            factors = gather_factors(factor_piece, bits)
            gate = advance(gate_anchor, gate_moment, rebuild(factors, basis))
            new_gate_anchor, new_gate_moment = gate
    received, mixed_received = parts[: len(spans)], parts[len(spans) :]
    new_norm_anchor, new_norm_moment = norm_finish(
        norm_anchor, norm_local[0], norm_moment, norm_received
    )

    moment_next = []
    for (start, size), part in zip(spans, received):
        old = down_moment[start : start + size]
        moment_next.append(
            momentum * old
            + rows_of(down_anchor, own + start, size)
            - 0.5 * (rows_of(local, own + start, size) + part)
        )
        value = rows_of(anchor_next, own + start, size) + ((rate / 2) * part - decay * old)
        anchor_next = lax.dynamic_update_slice_in_dim(anchor_next, value, own + start, 0)
    for i, ((start, size), part) in enumerate(zip(mixed_spans, mixed_received)):
        if i == pinned:
            anchor_next = add_rows(anchor_next, part, start, half)
        else:
            value = rows_of(anchor_next, other + start, size) + part
            anchor_next = lax.dynamic_update_slice_in_dim(anchor_next, value, other + start, 0)
    return (
        anchor_next,
        lax.concatenate(moment_next, 0),
        new_norm_anchor,
        new_norm_moment,
        new_gate_anchor,
        new_gate_moment,
    )


def solution(mesh):
    placed = (
        P("shard", "tensor"),
        P("group", "shard", "tensor"),
        P(("shard", "group"), "tensor"),
        P(None, ("shard", "tensor")),
        P("group", None, ("shard", "tensor")),
        P("group", ("shard", "tensor")),
        P("tensor", "shard"),
        P("group", "tensor", "shard"),
        P("tensor", "shard"),
        P(None, "shard"),
    )
    return jax.shard_map(
        body,
        mesh=mesh,
        in_specs=placed,
        out_specs=(
            P("shard", "tensor"),
            P(("shard", "group"), "tensor"),
            P(None, ("shard", "tensor")),
            P("group", ("shard", "tensor")),
            P("tensor", "shard"),
            P("tensor", "shard"),
        ),
        check_vma=False,
    )
```

```python
import functools

import jax
import jax.numpy as jnp
from jax import lax
from jax.experimental import pallas as pl
from jax.experimental.pallas import tpu as pltpu
from jax.sharding import PartitionSpec as P

outer_rate = 0.7
momentum = 0.9
rate = outer_rate * (1 + momentum)
decay = outer_rate * momentum * momentum
first_sizes = (1, 7, 12, 12)
last_sizes = (8, 8, 5, 5, 4, 2)
window = 3
gate_before = 6
pinned = 4


def advance(anchor, moment, delta):
    moment_next = momentum * moment + delta
    anchor_next = anchor - outer_rate * (delta + momentum * moment_next)
    return (anchor_next, moment_next)


def rebuild(factors, factor_basis):
    return lax.dot_general(
        factors, factor_basis, (((0,), (0,)), ((), ())), precision=lax.Precision.HIGHEST
    )


def swap(array):
    return lax.ppermute(array, "group", [(0, 1), (1, 0)])


def across(array, k):
    shards = lax.axis_size("shard")
    return lax.ppermute(array, "shard", [(i, i ^ k) for i in range(shards)])


def after(array, *earlier):
    return lax.optimization_barrier((array, *earlier))[0]


def pieces(half, sizes):
    unit = half // sum(sizes)
    start = 0
    for size in sizes:
        yield start * unit, size * unit
        start += size


def add_kernel(start, half, part, _, total, rows, sem):
    other = (1 - lax.axis_index("group")) * half
    span = total.at[pl.ds(pl.multiple_of(other + start, 8), part.shape[0])]
    read = pltpu.make_async_copy(span, rows, sem)
    read.start()
    read.wait()
    rows[...] += part[...]
    write = pltpu.make_async_copy(rows, span, sem)
    write.start()
    write.wait()


def add_rows(total, part, start, half):
    return pl.pallas_call(
        functools.partial(add_kernel, start, half),
        out_shape=jax.ShapeDtypeStruct(total.shape, total.dtype),
        in_specs=[
            pl.BlockSpec(memory_space=pltpu.VMEM),
            pl.BlockSpec(memory_space=pltpu.HBM),
        ],
        out_specs=pl.BlockSpec(memory_space=pltpu.HBM),
        scratch_shapes=[pltpu.VMEM(part.shape, part.dtype), pltpu.SemaphoreType.DMA],
        input_output_aliases={1: 0},
        cost_estimate=pl.CostEstimate(
            flops=part.size, bytes_accessed=12 * part.size, transcendentals=0
        ),
    )(part, total)


def scatter_factors(value, bits):
    for bit in bits:
        rest = value.shape[0] // 2
        value = value[:rest] + across(value[rest:], bit)
    return value


def gather_factors(value, bits):
    for bit in reversed(bits):
        value = lax.concatenate([value, across(value, bit)], 0)
    return value


def mine_of(shape, half):
    return lax.broadcasted_iota(jnp.int32, shape, 0) // half == lax.axis_index("group")


def norm_message(local, moment):
    wide = lax.concatenate([moment, moment], 0)
    mixed = (rate / 2) * local - decay * wide
    return jnp.where(mine_of(local.shape, moment.shape[0]), mixed, local)


def norm_finish(anchor, local, moment, received):
    half = moment.shape[0]
    wide = lax.concatenate([moment, moment], 0)
    mine = mine_of(anchor.shape, half)
    anchor_next = (1 - rate) * anchor + (rate / 2) * local
    anchor_next += jnp.where(mine, (rate / 2) * received - decay * wide, received)
    step = anchor - 0.5 * (local + received)
    own = lax.axis_index("group") * half
    return anchor_next, momentum * moment + lax.dynamic_slice_in_dim(step, own, half, 0)


def body(
    down_anchor,
    down_local,
    down_moment,
    norm_anchor,
    norm_local,
    norm_moment,
    gate_anchor,
    gate_local,
    gate_moment,
    factor_basis,
):
    groups = lax.axis_size("group")
    group_index = lax.axis_index("group")
    local = down_local[0]
    half = down_moment.shape[0]
    own = group_index * half
    other = half - own

    def rows_of(array, start, size):
        return lax.dynamic_slice_in_dim(array, start, size, 0)

    spans = list(pieces(half, first_sizes))
    mixed_spans = list(pieces(half, last_sizes))

    shards = lax.axis_size("shard")
    bits = [1 << n for n in range(shards.bit_length() - 1)]
    masks = [0]
    for bit in reversed(bits):
        masks += [mask | bit for mask in masks]
    block = factor_basis.shape[0] // shards
    basis = lax.concatenate(
        [rows_of(factor_basis, (lax.axis_index("shard") ^ mask) * block, block) for mask in masks],
        0,
    )
    gate_diff = gate_anchor - gate_local[0]
    partial_factors = lax.dot_general(
        basis, gate_diff, (((1,), (1,)), ((), ())), precision=lax.Precision.HIGHEST
    )
    factor_piece = scatter_factors(partial_factors, bits)
    factor_other = swap(factor_piece)

    parts = []
    cut = local
    for i, (start, size) in enumerate(spans + mixed_spans):
        if i < len(spans):
            part = rows_of(cut, other + start, size)
            if i < window:
                cut = after(local, part)
        else:
            part = mixed[start : start + size]
        ties = [parts[i - window]] if i >= window else []
        if i == gate_before:
            ties += gate
        parts.append(swap(after(part, *ties)))
        if i == 0:
            mixed = (rate / 2) * rows_of(local, own, half) - decay * after(down_moment, parts[0])
            anchor_next = (1 - rate) * after(down_anchor, parts[0]) + (rate / 2) * local
            norm_sent = after(norm_message(norm_local[0], norm_moment), parts[0])
            norm_received = swap(norm_sent)
        if i == len(spans) - 1:
            norm_received = after(norm_received, parts[i])
            factor_piece = (factor_piece + after(factor_other, parts[i])) / groups
            factors = gather_factors(factor_piece, bits)
            gate = advance(gate_anchor, gate_moment, rebuild(factors, basis))
            new_gate_anchor, new_gate_moment = gate
    received, mixed_received = parts[: len(spans)], parts[len(spans) :]
    new_norm_anchor, new_norm_moment = norm_finish(
        norm_anchor, norm_local[0], norm_moment, norm_received
    )

    start, size = mixed_spans[-1]
    last_base = after(rows_of(anchor_next, other + start, size), parts[-3])
    moment_next = []
    for (start, size), part in zip(spans, received):
        old = down_moment[start : start + size]
        moment_next.append(
            momentum * old
            + rows_of(down_anchor, own + start, size)
            - 0.5 * (rows_of(local, own + start, size) + part)
        )
        value = rows_of(anchor_next, own + start, size) + ((rate / 2) * part - decay * old)
        anchor_next = lax.dynamic_update_slice_in_dim(anchor_next, value, own + start, 0)
    for i, ((start, size), part) in enumerate(zip(mixed_spans, mixed_received)):
        if i == pinned:
            anchor_next = add_rows(anchor_next, part, start, half)
        else:
            value = last_base if i == len(mixed_spans) - 1 else rows_of(anchor_next, other + start, size)
            value = value + part
            anchor_next = lax.dynamic_update_slice_in_dim(anchor_next, value, other + start, 0)
    return (
        anchor_next,
        lax.concatenate(moment_next, 0),
        new_norm_anchor,
        new_norm_moment,
        new_gate_anchor,
        new_gate_moment,
    )


def solution(mesh):
    placed = (
        P("shard", "tensor"),
        P("group", "shard", "tensor"),
        P(("shard", "group"), "tensor"),
        P(None, ("shard", "tensor")),
        P("group", None, ("shard", "tensor")),
        P("group", ("shard", "tensor")),
        P("tensor", "shard"),
        P("group", "tensor", "shard"),
        P("tensor", "shard"),
        P(None, "shard"),
    )
    return jax.shard_map(
        body,
        mesh=mesh,
        in_specs=placed,
        out_specs=(
            P("shard", "tensor"),
            P(("shard", "group"), "tensor"),
            P(None, ("shard", "tensor")),
            P("group", ("shard", "tensor")),
            P("tensor", "shard"),
            P("tensor", "shard"),
        ),
        check_vma=False,
    )
```

```python
import functools

import jax
import jax.numpy as jnp
from jax import lax
from jax.experimental import pallas as pl
from jax.experimental.pallas import tpu as pltpu
from jax.sharding import PartitionSpec as P

outer_rate = 0.7
momentum = 0.9
rate = outer_rate * (1 + momentum)
decay = outer_rate * momentum * momentum
first_sizes = (1, 5, 13, 13)
last_sizes = (8, 8, 5, 5, 4, 2)
window = 3
gate_before = 6
pinned = 4


def advance(anchor, moment, delta):
    moment_next = momentum * moment + delta
    anchor_next = anchor - outer_rate * (delta + momentum * moment_next)
    return (anchor_next, moment_next)


def rebuild(factors, factor_basis):
    return lax.dot_general(
        factors, factor_basis, (((0,), (0,)), ((), ())), precision=lax.Precision.HIGHEST
    )


def swap(array):
    return lax.ppermute(array, "group", [(0, 1), (1, 0)])


def across(array, k):
    shards = lax.axis_size("shard")
    return lax.ppermute(array, "shard", [(i, i ^ k) for i in range(shards)])


def after(array, *earlier):
    return lax.optimization_barrier((array, *earlier))[0]


def pieces(half, sizes):
    unit = half // sum(sizes)
    start = 0
    for size in sizes:
        yield start * unit, size * unit
        start += size


def add_kernel(start, half, part, _, total, rows, sem):
    other = (1 - lax.axis_index("group")) * half
    span = total.at[pl.ds(pl.multiple_of(other + start, 8), part.shape[0])]
    read = pltpu.make_async_copy(span, rows, sem)
    read.start()
    read.wait()
    rows[...] += part[...]
    write = pltpu.make_async_copy(rows, span, sem)
    write.start()
    write.wait()


def add_rows(total, part, start, half):
    return pl.pallas_call(
        functools.partial(add_kernel, start, half),
        out_shape=jax.ShapeDtypeStruct(total.shape, total.dtype),
        in_specs=[
            pl.BlockSpec(memory_space=pltpu.VMEM),
            pl.BlockSpec(memory_space=pltpu.HBM),
        ],
        out_specs=pl.BlockSpec(memory_space=pltpu.HBM),
        scratch_shapes=[pltpu.VMEM(part.shape, part.dtype), pltpu.SemaphoreType.DMA],
        input_output_aliases={1: 0},
        cost_estimate=pl.CostEstimate(
            flops=part.size, bytes_accessed=12 * part.size, transcendentals=0
        ),
    )(part, total)


def scatter_factors(value, bits):
    for bit in bits:
        rest = value.shape[0] // 2
        value = value[:rest] + across(value[rest:], bit)
    return value


def gather_factors(value, bits):
    for bit in reversed(bits):
        value = lax.concatenate([value, across(value, bit)], 0)
    return value


def mine_of(shape, half):
    return lax.broadcasted_iota(jnp.int32, shape, 0) // half == lax.axis_index("group")


def norm_message(local, moment):
    wide = lax.concatenate([moment, moment], 0)
    mixed = (rate / 2) * local - decay * wide
    return jnp.where(mine_of(local.shape, moment.shape[0]), mixed, local)


def norm_finish(anchor, local, moment, received):
    half = moment.shape[0]
    wide = lax.concatenate([moment, moment], 0)
    mine = mine_of(anchor.shape, half)
    anchor_next = (1 - rate) * anchor + (rate / 2) * local
    anchor_next += jnp.where(mine, (rate / 2) * received - decay * wide, received)
    step = anchor - 0.5 * (local + received)
    own = lax.axis_index("group") * half
    return anchor_next, momentum * moment + lax.dynamic_slice_in_dim(step, own, half, 0)


def body(
    down_anchor,
    down_local,
    down_moment,
    norm_anchor,
    norm_local,
    norm_moment,
    gate_anchor,
    gate_local,
    gate_moment,
    factor_basis,
):
    groups = lax.axis_size("group")
    group_index = lax.axis_index("group")
    local = down_local[0]
    half = down_moment.shape[0]
    own = group_index * half
    other = half - own

    def rows_of(array, start, size):
        return lax.dynamic_slice_in_dim(array, start, size, 0)

    spans = list(pieces(half, first_sizes))
    mixed_spans = list(pieces(half, last_sizes))

    shards = lax.axis_size("shard")
    bits = [1 << n for n in range(shards.bit_length() - 1)]
    masks = [0]
    for bit in reversed(bits):
        masks += [mask | bit for mask in masks]
    block = factor_basis.shape[0] // shards
    basis = lax.concatenate(
        [rows_of(factor_basis, (lax.axis_index("shard") ^ mask) * block, block) for mask in masks],
        0,
    )
    gate_diff = gate_anchor - gate_local[0]
    partial_factors = lax.dot_general(
        basis, gate_diff, (((1,), (1,)), ((), ())), precision=lax.Precision.HIGHEST
    )
    factor_piece = scatter_factors(partial_factors, bits)
    factor_other = swap(factor_piece)

    parts = []
    cut = local
    for i, (start, size) in enumerate(spans + mixed_spans):
        if i < len(spans):
            part = rows_of(cut, other + start, size)
            if i < window:
                cut = after(local, part)
        else:
            part = mixed[start : start + size]
        ties = [parts[i - window]] if i >= window else []
        if i == gate_before:
            ties += gate
        parts.append(swap(after(part, *ties)))
        if i == 0:
            mixed = (rate / 2) * rows_of(local, own, half) - decay * after(down_moment, parts[0])
            anchor_next = (1 - rate) * after(down_anchor, parts[0]) + (rate / 2) * local
            norm_sent = after(norm_message(norm_local[0], norm_moment), parts[0])
            norm_received = swap(norm_sent)
        if i == len(spans) - 1:
            norm_received = after(norm_received, parts[i])
            factor_piece = (factor_piece + after(factor_other, parts[i])) / groups
            factors = gather_factors(factor_piece, bits)
            gate = advance(gate_anchor, gate_moment, rebuild(factors, basis))
            new_gate_anchor, new_gate_moment = gate
    received, mixed_received = parts[: len(spans)], parts[len(spans) :]
    new_norm_anchor, new_norm_moment = norm_finish(
        norm_anchor, norm_local[0], norm_moment, norm_received
    )

    start, size = mixed_spans[-1]
    last_base = after(rows_of(anchor_next, other + start, size), parts[-3])
    moment_next = []
    for (start, size), part in zip(spans, received):
        old = down_moment[start : start + size]
        moment_next.append(
            momentum * old
            + rows_of(down_anchor, own + start, size)
            - 0.5 * (rows_of(local, own + start, size) + part)
        )
        value = rows_of(anchor_next, own + start, size) + ((rate / 2) * part - decay * old)
        anchor_next = lax.dynamic_update_slice_in_dim(anchor_next, value, own + start, 0)
    for i, ((start, size), part) in enumerate(zip(mixed_spans, mixed_received)):
        if i == pinned:
            anchor_next = add_rows(anchor_next, part, start, half)
        else:
            value = last_base if i == len(mixed_spans) - 1 else rows_of(anchor_next, other + start, size)
            value = value + part
            anchor_next = lax.dynamic_update_slice_in_dim(anchor_next, value, other + start, 0)
    return (
        anchor_next,
        lax.concatenate(moment_next, 0),
        new_norm_anchor,
        new_norm_moment,
        new_gate_anchor,
        new_gate_moment,
    )


def solution(mesh):
    placed = (
        P("shard", "tensor"),
        P("group", "shard", "tensor"),
        P(("shard", "group"), "tensor"),
        P(None, ("shard", "tensor")),
        P("group", None, ("shard", "tensor")),
        P("group", ("shard", "tensor")),
        P("tensor", "shard"),
        P("group", "tensor", "shard"),
        P("tensor", "shard"),
        P(None, "shard"),
    )
    return jax.shard_map(
        body,
        mesh=mesh,
        in_specs=placed,
        out_specs=(
            P("shard", "tensor"),
            P(("shard", "group"), "tensor"),
            P(None, ("shard", "tensor")),
            P("group", ("shard", "tensor")),
            P("tensor", "shard"),
            P("tensor", "shard"),
        ),
        check_vma=False,
    )
```

```python
import functools

import jax
import jax.numpy as jnp
from jax import lax
from jax.experimental import pallas as pl
from jax.experimental.pallas import tpu as pltpu
from jax.sharding import PartitionSpec as P

outer_rate = 0.7
momentum = 0.9
rate = outer_rate * (1 + momentum)
decay = outer_rate * momentum * momentum
first_sizes = (1, 6, 12, 13)
last_sizes = (8, 8, 5, 5, 4, 2)
window = 3
gate_before = 6
pinned = 4


def advance(anchor, moment, delta):
    moment_next = momentum * moment + delta
    anchor_next = anchor - outer_rate * (delta + momentum * moment_next)
    return (anchor_next, moment_next)


def rebuild(factors, factor_basis):
    return lax.dot_general(
        factors, factor_basis, (((0,), (0,)), ((), ())), precision=lax.Precision.HIGHEST
    )


def swap(array):
    return lax.ppermute(array, "group", [(0, 1), (1, 0)])


def across(array, k):
    shards = lax.axis_size("shard")
    return lax.ppermute(array, "shard", [(i, i ^ k) for i in range(shards)])


def after(array, *earlier):
    return lax.optimization_barrier((array, *earlier))[0]


def pieces(half, sizes):
    unit = half // sum(sizes)
    start = 0
    for size in sizes:
        yield start * unit, size * unit
        start += size


def add_kernel(start, half, part, _, total, rows, sem):
    other = (1 - lax.axis_index("group")) * half
    span = total.at[pl.ds(pl.multiple_of(other + start, 8), part.shape[0])]
    read = pltpu.make_async_copy(span, rows, sem)
    read.start()
    read.wait()
    rows[...] += part[...]
    write = pltpu.make_async_copy(rows, span, sem)
    write.start()
    write.wait()


def add_rows(total, part, start, half):
    return pl.pallas_call(
        functools.partial(add_kernel, start, half),
        out_shape=jax.ShapeDtypeStruct(total.shape, total.dtype),
        in_specs=[
            pl.BlockSpec(memory_space=pltpu.VMEM),
            pl.BlockSpec(memory_space=pltpu.HBM),
        ],
        out_specs=pl.BlockSpec(memory_space=pltpu.HBM),
        scratch_shapes=[pltpu.VMEM(part.shape, part.dtype), pltpu.SemaphoreType.DMA],
        input_output_aliases={1: 0},
        cost_estimate=pl.CostEstimate(
            flops=part.size, bytes_accessed=12 * part.size, transcendentals=0
        ),
    )(part, total)


def scatter_factors(value, bits):
    for bit in bits:
        rest = value.shape[0] // 2
        value = value[:rest] + across(value[rest:], bit)
    return value


def gather_factors(value, bits):
    for bit in reversed(bits):
        value = lax.concatenate([value, across(value, bit)], 0)
    return value


def mine_of(shape, half):
    return lax.broadcasted_iota(jnp.int32, shape, 0) // half == lax.axis_index("group")


def norm_message(local, moment):
    wide = lax.concatenate([moment, moment], 0)
    mixed = (rate / 2) * local - decay * wide
    return jnp.where(mine_of(local.shape, moment.shape[0]), mixed, local)


def norm_finish(anchor, local, moment, received):
    half = moment.shape[0]
    wide = lax.concatenate([moment, moment], 0)
    mine = mine_of(anchor.shape, half)
    anchor_next = (1 - rate) * anchor + (rate / 2) * local
    anchor_next += jnp.where(mine, (rate / 2) * received - decay * wide, received)
    step = anchor - 0.5 * (local + received)
    own = lax.axis_index("group") * half
    return anchor_next, momentum * moment + lax.dynamic_slice_in_dim(step, own, half, 0)


def body(
    down_anchor,
    down_local,
    down_moment,
    norm_anchor,
    norm_local,
    norm_moment,
    gate_anchor,
    gate_local,
    gate_moment,
    factor_basis,
):
    groups = lax.axis_size("group")
    group_index = lax.axis_index("group")
    local = down_local[0]
    half = down_moment.shape[0]
    own = group_index * half
    other = half - own

    def rows_of(array, start, size):
        return lax.dynamic_slice_in_dim(array, start, size, 0)

    spans = list(pieces(half, first_sizes))
    mixed_spans = list(pieces(half, last_sizes))

    shards = lax.axis_size("shard")
    bits = [1 << n for n in range(shards.bit_length() - 1)]
    masks = [0]
    for bit in reversed(bits):
        masks += [mask | bit for mask in masks]
    block = factor_basis.shape[0] // shards
    basis = lax.concatenate(
        [rows_of(factor_basis, (lax.axis_index("shard") ^ mask) * block, block) for mask in masks],
        0,
    )
    gate_diff = gate_anchor - gate_local[0]
    partial_factors = lax.dot_general(
        basis, gate_diff, (((1,), (1,)), ((), ())), precision=lax.Precision.HIGHEST
    )
    factor_piece = scatter_factors(partial_factors, bits)
    factor_other = swap(factor_piece)

    parts = []
    cut = local
    for i, (start, size) in enumerate(spans + mixed_spans):
        if i < len(spans):
            part = rows_of(cut, other + start, size)
            if i < window:
                cut = after(local, part)
        else:
            part = mixed[start : start + size]
        ties = [parts[i - window]] if i >= window else []
        if i == gate_before:
            ties += gate
        parts.append(swap(after(part, *ties)))
        if i == 0:
            mixed = (rate / 2) * rows_of(local, own, half) - decay * after(down_moment, parts[0])
            anchor_next = (1 - rate) * after(down_anchor, parts[0]) + (rate / 2) * local
            norm_sent = after(norm_message(norm_local[0], norm_moment), parts[0])
            norm_received = swap(norm_sent)
        if i == len(spans) - 1:
            norm_received = after(norm_received, parts[i])
            factor_piece = (factor_piece + after(factor_other, parts[i])) / groups
            factors = gather_factors(factor_piece, bits)
            gate = advance(gate_anchor, gate_moment, rebuild(factors, basis))
            new_gate_anchor, new_gate_moment = gate
    received, mixed_received = parts[: len(spans)], parts[len(spans) :]
    new_norm_anchor, new_norm_moment = norm_finish(
        norm_anchor, norm_local[0], norm_moment, norm_received
    )

    start, size = mixed_spans[-1]
    last_base = after(rows_of(anchor_next, other + start, size), parts[-3])
    moment_next = []
    for (start, size), part in zip(spans, received):
        old = down_moment[start : start + size]
        moment_next.append(
            momentum * old
            + rows_of(down_anchor, own + start, size)
            - 0.5 * (rows_of(local, own + start, size) + part)
        )
        value = rows_of(anchor_next, own + start, size) + ((rate / 2) * part - decay * old)
        anchor_next = lax.dynamic_update_slice_in_dim(anchor_next, value, own + start, 0)
    for i, ((start, size), part) in enumerate(zip(mixed_spans, mixed_received)):
        if i == pinned:
            anchor_next = add_rows(anchor_next, part, start, half)
        else:
            value = last_base if i == len(mixed_spans) - 1 else rows_of(anchor_next, other + start, size)
            value = value + part
            anchor_next = lax.dynamic_update_slice_in_dim(anchor_next, value, other + start, 0)
    return (
        anchor_next,
        lax.concatenate(moment_next, 0),
        new_norm_anchor,
        new_norm_moment,
        new_gate_anchor,
        new_gate_moment,
    )


def solution(mesh):
    placed = (
        P("shard", "tensor"),
        P("group", "shard", "tensor"),
        P(("shard", "group"), "tensor"),
        P(None, ("shard", "tensor")),
        P("group", None, ("shard", "tensor")),
        P("group", ("shard", "tensor")),
        P("tensor", "shard"),
        P("group", "tensor", "shard"),
        P("tensor", "shard"),
        P(None, "shard"),
    )
    return jax.shard_map(
        body,
        mesh=mesh,
        in_specs=placed,
        out_specs=(
            P("shard", "tensor"),
            P(("shard", "group"), "tensor"),
            P(None, ("shard", "tensor")),
            P("group", ("shard", "tensor")),
            P("tensor", "shard"),
            P("tensor", "shard"),
        ),
        check_vma=False,
    )
```

```python
import functools

import jax
import jax.numpy as jnp
from jax import lax
from jax.experimental import pallas as pl
from jax.experimental.pallas import tpu as pltpu
from jax.sharding import PartitionSpec as P

outer_rate = 0.7
momentum = 0.9
rate = outer_rate * (1 + momentum)
decay = outer_rate * momentum * momentum
first_sizes = (1, 6, 12, 13)
last_sizes = (8, 8, 5, 5, 4, 2)
window = 3
gate_before = 6
pinned = 4


def advance(anchor, moment, delta):
    moment_next = momentum * moment + delta
    anchor_next = anchor - outer_rate * (delta + momentum * moment_next)
    return (anchor_next, moment_next)


def rebuild(factors, factor_basis):
    return lax.dot_general(
        factors, factor_basis, (((0,), (0,)), ((), ())), precision=lax.Precision.HIGHEST
    )


def swap(array):
    return lax.ppermute(array, "group", [(0, 1), (1, 0)])


def across(array, k):
    shards = lax.axis_size("shard")
    return lax.ppermute(array, "shard", [(i, i ^ k) for i in range(shards)])


def after(array, *earlier):
    return lax.optimization_barrier((array, *earlier))[0]


def pieces(half, sizes):
    unit = half // sum(sizes)
    start = 0
    for size in sizes:
        yield start * unit, size * unit
        start += size


def add_kernel(start, half, part, _, total, rows, sem):
    other = (1 - lax.axis_index("group")) * half
    span = total.at[pl.ds(pl.multiple_of(other + start, 8), part.shape[0])]
    read = pltpu.make_async_copy(span, rows, sem)
    read.start()
    read.wait()
    rows[...] += part[...]
    write = pltpu.make_async_copy(rows, span, sem)
    write.start()
    write.wait()


def add_rows(total, part, start, half):
    return pl.pallas_call(
        functools.partial(add_kernel, start, half),
        out_shape=jax.ShapeDtypeStruct(total.shape, total.dtype),
        in_specs=[
            pl.BlockSpec(memory_space=pltpu.VMEM),
            pl.BlockSpec(memory_space=pltpu.HBM),
        ],
        out_specs=pl.BlockSpec(memory_space=pltpu.HBM),
        scratch_shapes=[pltpu.VMEM(part.shape, part.dtype), pltpu.SemaphoreType.DMA],
        input_output_aliases={1: 0},
        cost_estimate=pl.CostEstimate(
            flops=part.size, bytes_accessed=12 * part.size, transcendentals=0
        ),
    )(part, total)


def scatter_factors(value, bits):
    for bit in bits:
        rest = value.shape[0] // 2
        value = value[:rest] + across(value[rest:], bit)
    return value


def gather_factors(value, bits):
    for bit in reversed(bits):
        value = lax.concatenate([value, across(value, bit)], 0)
    return value


def mine_of(shape, half):
    return lax.broadcasted_iota(jnp.int32, shape, 0) // half == lax.axis_index("group")


def norm_message(local, moment):
    wide = lax.concatenate([moment, moment], 0)
    mixed = (rate / 2) * local - decay * wide
    return jnp.where(mine_of(local.shape, moment.shape[0]), mixed, local)


def norm_finish(anchor, local, moment, received):
    half = moment.shape[0]
    wide = lax.concatenate([moment, moment], 0)
    mine = mine_of(anchor.shape, half)
    anchor_next = (1 - rate) * anchor + (rate / 2) * local
    anchor_next += jnp.where(mine, (rate / 2) * received - decay * wide, received)
    step = anchor - 0.5 * (local + received)
    own = lax.axis_index("group") * half
    return anchor_next, momentum * moment + lax.dynamic_slice_in_dim(step, own, half, 0)


def body(
    down_anchor,
    down_local,
    down_moment,
    norm_anchor,
    norm_local,
    norm_moment,
    gate_anchor,
    gate_local,
    gate_moment,
    factor_basis,
):
    groups = lax.axis_size("group")
    group_index = lax.axis_index("group")
    local = down_local[0]
    half = down_moment.shape[0]
    own = group_index * half
    other = half - own

    def rows_of(array, start, size):
        return lax.dynamic_slice_in_dim(array, start, size, 0)

    spans = list(pieces(half, first_sizes))
    mixed_spans = list(pieces(half, last_sizes))

    shards = lax.axis_size("shard")
    bits = [1 << n for n in range(shards.bit_length() - 1)]
    masks = [0]
    for bit in reversed(bits):
        masks += [mask | bit for mask in masks]
    block = factor_basis.shape[0] // shards
    basis = lax.concatenate(
        [rows_of(factor_basis, (lax.axis_index("shard") ^ mask) * block, block) for mask in masks],
        0,
    )
    gate_diff = gate_anchor - gate_local[0]
    partial_factors = lax.dot_general(
        basis, gate_diff, (((1,), (1,)), ((), ())), precision=lax.Precision.HIGHEST
    )
    factor_piece = scatter_factors(partial_factors, bits)
    factor_other = swap(factor_piece)

    parts = []
    cut = local
    for i, (start, size) in enumerate(spans + mixed_spans):
        if i < len(spans):
            part = rows_of(cut, other + start, size)
            if i < window:
                cut = after(local, part)
        else:
            part = mixed[start : start + size]
        if i == len(spans) + len(mixed_spans) - 1:
            part = settled[start - settled_from :]
        ties = [parts[i - window]] if i >= window else []
        if i == gate_before:
            ties += gate
        parts.append(swap(after(part, *ties)))
        if i == 0:
            mixed = (rate / 2) * rows_of(local, own, half) - decay * after(down_moment, parts[0])
            anchor_next = (1 - rate) * after(down_anchor, parts[0]) + (rate / 2) * local
            norm_sent = after(norm_message(norm_local[0], norm_moment), parts[0])
            norm_received = swap(norm_sent)
        if i == len(spans) - 1:
            norm_received = after(norm_received, parts[i])
            settled_from = start
            settled = rows_of(anchor_next, own + start, size)
            settled += (rate / 2) * parts[i] - decay * down_moment[start:]
            factor_piece = (factor_piece + after(factor_other, parts[i])) / groups
            factors = gather_factors(factor_piece, bits)
            gate = advance(gate_anchor, gate_moment, rebuild(factors, basis))
            new_gate_anchor, new_gate_moment = gate
    received, mixed_received = parts[: len(spans)], parts[len(spans) :]
    new_norm_anchor, new_norm_moment = norm_finish(
        norm_anchor, norm_local[0], norm_moment, norm_received
    )

    moment_next = []
    for (start, size), part in zip(spans, received):
        old = down_moment[start : start + size]
        moment_next.append(
            momentum * old
            + rows_of(down_anchor, own + start, size)
            - 0.5 * (rows_of(local, own + start, size) + part)
        )
        value = rows_of(anchor_next, own + start, size) + ((rate / 2) * part - decay * old)
        anchor_next = lax.dynamic_update_slice_in_dim(anchor_next, value, own + start, 0)
    for i, ((start, size), part) in enumerate(zip(mixed_spans, mixed_received)):
        if i == pinned:
            anchor_next = add_rows(anchor_next, part, start, half)
        else:
            value = part
            if i < len(mixed_spans) - 1:
                value = value + rows_of(anchor_next, other + start, size)
            anchor_next = lax.dynamic_update_slice_in_dim(anchor_next, value, other + start, 0)
    return (
        anchor_next,
        lax.concatenate(moment_next, 0),
        new_norm_anchor,
        new_norm_moment,
        new_gate_anchor,
        new_gate_moment,
    )


def solution(mesh):
    placed = (
        P("shard", "tensor"),
        P("group", "shard", "tensor"),
        P(("shard", "group"), "tensor"),
        P(None, ("shard", "tensor")),
        P("group", None, ("shard", "tensor")),
        P("group", ("shard", "tensor")),
        P("tensor", "shard"),
        P("group", "tensor", "shard"),
        P("tensor", "shard"),
        P(None, "shard"),
    )
    return jax.shard_map(
        body,
        mesh=mesh,
        in_specs=placed,
        out_specs=(
            P("shard", "tensor"),
            P(("shard", "group"), "tensor"),
            P(None, ("shard", "tensor")),
            P("group", ("shard", "tensor")),
            P("tensor", "shard"),
            P("tensor", "shard"),
        ),
        check_vma=False,
    )
```

```python
import functools

import jax
import jax.numpy as jnp
from jax import lax
from jax.experimental import pallas as pl
from jax.experimental.pallas import tpu as pltpu
from jax.sharding import PartitionSpec as P

outer_rate = 0.7
momentum = 0.9
rate = outer_rate * (1 + momentum)
decay = outer_rate * momentum * momentum
first_sizes = (1, 6, 12, 13)
last_sizes = (8, 8, 5, 5, 4, 2)
window = 3
gate_before = 6
pinned = 4


def advance(anchor, moment, delta):
    moment_next = momentum * moment + delta
    anchor_next = anchor - outer_rate * (delta + momentum * moment_next)
    return (anchor_next, moment_next)


def rebuild(factors, factor_basis):
    return lax.dot_general(
        factors, factor_basis, (((0,), (0,)), ((), ())), precision=lax.Precision.HIGHEST
    )


def swap(array):
    return lax.ppermute(array, "group", [(0, 1), (1, 0)])


def across(array, k):
    shards = lax.axis_size("shard")
    return lax.ppermute(array, "shard", [(i, i ^ k) for i in range(shards)])


def after(array, *earlier):
    return lax.optimization_barrier((array, *earlier))[0]


def pieces(half, sizes):
    unit = half // sum(sizes)
    start = 0
    for size in sizes:
        yield start * unit, size * unit
        start += size


def add_kernel(start, half, part, _, total, rows, sem):
    other = (1 - lax.axis_index("group")) * half
    span = total.at[pl.ds(pl.multiple_of(other + start, 8), part.shape[0])]
    read = pltpu.make_async_copy(span, rows, sem)
    read.start()
    read.wait()
    rows[...] += part[...]
    write = pltpu.make_async_copy(rows, span, sem)
    write.start()
    write.wait()


def add_rows(total, part, start, half):
    return pl.pallas_call(
        functools.partial(add_kernel, start, half),
        out_shape=jax.ShapeDtypeStruct(total.shape, total.dtype),
        in_specs=[
            pl.BlockSpec(memory_space=pltpu.VMEM),
            pl.BlockSpec(memory_space=pltpu.HBM),
        ],
        out_specs=pl.BlockSpec(memory_space=pltpu.HBM),
        scratch_shapes=[pltpu.VMEM(part.shape, part.dtype), pltpu.SemaphoreType.DMA],
        input_output_aliases={1: 0},
        cost_estimate=pl.CostEstimate(
            flops=part.size, bytes_accessed=12 * part.size, transcendentals=0
        ),
    )(part, total)


def scatter_factors(value, bits):
    for bit in bits:
        rest = value.shape[0] // 2
        value = value[:rest] + across(value[rest:], bit)
    return value


def gather_factors(value, bits):
    for bit in reversed(bits):
        value = lax.concatenate([value, across(value, bit)], 0)
    return value


def rows_of(array, start, size):
    return lax.dynamic_slice_in_dim(array, start, size, allow_negative_indices=False)


def put_rows(array, rows, start):
    return lax.dynamic_update_slice_in_dim(array, rows, start, 0, allow_negative_indices=False)


def mine_of(shape, half):
    return lax.broadcasted_iota(jnp.int32, shape, 0) // half == lax.axis_index("group")


def norm_message(local, moment):
    wide = lax.concatenate([moment, moment], 0)
    mixed = (rate / 2) * local - decay * wide
    return jnp.where(mine_of(local.shape, moment.shape[0]), mixed, local)


def norm_finish(anchor, local, moment, received):
    half = moment.shape[0]
    wide = lax.concatenate([moment, moment], 0)
    mine = mine_of(anchor.shape, half)
    anchor_next = (1 - rate) * anchor + (rate / 2) * local
    anchor_next += jnp.where(mine, (rate / 2) * received - decay * wide, received)
    step = anchor - 0.5 * (local + received)
    own = lax.axis_index("group") * half
    return anchor_next, momentum * moment + rows_of(step, own, half)


def body(
    down_anchor,
    down_local,
    down_moment,
    norm_anchor,
    norm_local,
    norm_moment,
    gate_anchor,
    gate_local,
    gate_moment,
    factor_basis,
):
    groups = lax.axis_size("group")
    group_index = lax.axis_index("group")
    local = down_local[0]
    half = down_moment.shape[0]
    own = group_index * half
    other = half - own

    spans = list(pieces(half, first_sizes))
    mixed_spans = list(pieces(half, last_sizes))

    shards = lax.axis_size("shard")
    bits = [1 << n for n in range(shards.bit_length() - 1)]
    masks = [0]
    for bit in reversed(bits):
        masks += [mask | bit for mask in masks]
    block = factor_basis.shape[0] // shards
    basis = lax.concatenate(
        [rows_of(factor_basis, (lax.axis_index("shard") ^ mask) * block, block) for mask in masks],
        0,
    )
    gate_diff = gate_anchor - gate_local[0]
    partial_factors = lax.dot_general(
        basis, gate_diff, (((1,), (1,)), ((), ())), precision=lax.Precision.HIGHEST
    )
    factor_piece = scatter_factors(partial_factors, bits)
    factor_other = swap(factor_piece)

    parts = []
    cut = local
    for i, (start, size) in enumerate(spans + mixed_spans):
        if i < len(spans):
            part = rows_of(cut, other + start, size)
            if i < window:
                cut = after(local, part)
        else:
            part = mixed[start : start + size]
        if i == len(spans) + len(mixed_spans) - 1:
            part = settled[start - settled_from :]
        ties = [parts[i - window]] if i >= window else []
        if i == gate_before:
            ties += gate
        parts.append(swap(after(part, *ties)))
        if i == 0:
            mixed = (rate / 2) * rows_of(local, own, half) - decay * after(down_moment, parts[0])
            anchor_next = (1 - rate) * after(down_anchor, parts[0]) + (rate / 2) * local
            norm_sent = after(norm_message(norm_local[0], norm_moment), parts[0])
            norm_received = swap(norm_sent)
        if i == len(spans) - 1:
            norm_received = after(norm_received, parts[i])
            settled_from = start
            settled = rows_of(anchor_next, own + start, size)
            settled += (rate / 2) * parts[i] - decay * down_moment[start:]
            factor_piece = (factor_piece + after(factor_other, parts[i])) / groups
            factors = gather_factors(factor_piece, bits)
            gate = advance(gate_anchor, gate_moment, rebuild(factors, basis))
            new_gate_anchor, new_gate_moment = gate
    received, mixed_received = parts[: len(spans)], parts[len(spans) :]
    new_norm_anchor, new_norm_moment = norm_finish(
        norm_anchor, norm_local[0], norm_moment, norm_received
    )

    moment_next = []
    for (start, size), part in zip(spans, received):
        old = down_moment[start : start + size]
        moment_next.append(
            momentum * old
            + rows_of(down_anchor, own + start, size)
            - 0.5 * (rows_of(local, own + start, size) + part)
        )
        value = rows_of(anchor_next, own + start, size) + ((rate / 2) * part - decay * old)
        anchor_next = put_rows(anchor_next, value, own + start)
    for i, ((start, size), part) in enumerate(zip(mixed_spans, mixed_received)):
        if i == pinned:
            anchor_next = add_rows(anchor_next, part, start, half)
        else:
            value = part
            if i < len(mixed_spans) - 1:
                value = value + rows_of(anchor_next, other + start, size)
            anchor_next = put_rows(anchor_next, value, other + start)
    return (
        anchor_next,
        lax.concatenate(moment_next, 0),
        new_norm_anchor,
        new_norm_moment,
        new_gate_anchor,
        new_gate_moment,
    )


def solution(mesh):
    placed = (
        P("shard", "tensor"),
        P("group", "shard", "tensor"),
        P(("shard", "group"), "tensor"),
        P(None, ("shard", "tensor")),
        P("group", None, ("shard", "tensor")),
        P("group", ("shard", "tensor")),
        P("tensor", "shard"),
        P("group", "tensor", "shard"),
        P("tensor", "shard"),
        P(None, "shard"),
    )
    return jax.shard_map(
        body,
        mesh=mesh,
        in_specs=placed,
        out_specs=(
            P("shard", "tensor"),
            P(("shard", "group"), "tensor"),
            P(None, ("shard", "tensor")),
            P("group", ("shard", "tensor")),
            P("tensor", "shard"),
            P("tensor", "shard"),
        ),
        check_vma=False,
    )
```

```python
import functools

import jax
import jax.numpy as jnp
from jax import lax
from jax.experimental import pallas as pl
from jax.experimental.pallas import tpu as pltpu
from jax.sharding import PartitionSpec as P

outer_rate = 0.7
momentum = 0.9
rate = outer_rate * (1 + momentum)
decay = outer_rate * momentum * momentum
first_sizes = (3, 11, 24, 26)
last_sizes = (8, 8, 5, 5, 4, 2)
window = 3
gate_before = 6
pinned = 4


def advance(anchor, moment, delta):
    moment_next = momentum * moment + delta
    anchor_next = anchor - outer_rate * (delta + momentum * moment_next)
    return (anchor_next, moment_next)


def rebuild(factors, factor_basis):
    return lax.dot_general(
        factors, factor_basis, (((0,), (0,)), ((), ())), precision=lax.Precision.HIGHEST
    )


def swap(array):
    return lax.ppermute(array, "group", [(0, 1), (1, 0)])


def across(array, k):
    shards = lax.axis_size("shard")
    return lax.ppermute(array, "shard", [(i, i ^ k) for i in range(shards)])


def after(array, *earlier):
    return lax.optimization_barrier((array, *earlier))[0]


def pieces(half, sizes):
    unit = half // sum(sizes)
    start = 0
    for size in sizes:
        yield start * unit, size * unit
        start += size


def add_kernel(start, half, part, _, total, rows, sem):
    other = (1 - lax.axis_index("group")) * half
    span = total.at[pl.ds(pl.multiple_of(other + start, 8), part.shape[0])]
    read = pltpu.make_async_copy(span, rows, sem)
    read.start()
    read.wait()
    rows[...] += part[...]
    write = pltpu.make_async_copy(rows, span, sem)
    write.start()
    write.wait()


def add_rows(total, part, start, half):
    return pl.pallas_call(
        functools.partial(add_kernel, start, half),
        out_shape=jax.ShapeDtypeStruct(total.shape, total.dtype),
        in_specs=[
            pl.BlockSpec(memory_space=pltpu.VMEM),
            pl.BlockSpec(memory_space=pltpu.HBM),
        ],
        out_specs=pl.BlockSpec(memory_space=pltpu.HBM),
        scratch_shapes=[pltpu.VMEM(part.shape, part.dtype), pltpu.SemaphoreType.DMA],
        input_output_aliases={1: 0},
        cost_estimate=pl.CostEstimate(
            flops=part.size, bytes_accessed=12 * part.size, transcendentals=0
        ),
    )(part, total)


def scatter_factors(value, bits):
    for bit in bits:
        rest = value.shape[0] // 2
        value = value[:rest] + across(value[rest:], bit)
    return value


def gather_factors(value, bits):
    for bit in reversed(bits):
        value = lax.concatenate([value, across(value, bit)], 0)
    return value


def rows_of(array, start, size):
    return lax.dynamic_slice_in_dim(array, start, size, allow_negative_indices=False)


def put_rows(array, rows, start):
    return lax.dynamic_update_slice_in_dim(array, rows, start, 0, allow_negative_indices=False)


def mine_of(shape, half):
    return lax.broadcasted_iota(jnp.int32, shape, 0) // half == lax.axis_index("group")


def norm_message(local, moment):
    wide = lax.concatenate([moment, moment], 0)
    mixed = (rate / 2) * local - decay * wide
    return jnp.where(mine_of(local.shape, moment.shape[0]), mixed, local)


def norm_finish(anchor, local, moment, received):
    half = moment.shape[0]
    wide = lax.concatenate([moment, moment], 0)
    mine = mine_of(anchor.shape, half)
    anchor_next = (1 - rate) * anchor + (rate / 2) * local
    anchor_next += jnp.where(mine, (rate / 2) * received - decay * wide, received)
    step = anchor - 0.5 * (local + received)
    own = lax.axis_index("group") * half
    return anchor_next, momentum * moment + rows_of(step, own, half)


def body(
    down_anchor,
    down_local,
    down_moment,
    norm_anchor,
    norm_local,
    norm_moment,
    gate_anchor,
    gate_local,
    gate_moment,
    factor_basis,
):
    groups = lax.axis_size("group")
    group_index = lax.axis_index("group")
    local = down_local[0]
    half = down_moment.shape[0]
    own = group_index * half
    other = half - own

    spans = list(pieces(half, first_sizes))
    mixed_spans = list(pieces(half, last_sizes))

    shards = lax.axis_size("shard")
    bits = [1 << n for n in range(shards.bit_length() - 1)]
    masks = [0]
    for bit in reversed(bits):
        masks += [mask | bit for mask in masks]
    block = factor_basis.shape[0] // shards
    basis = lax.concatenate(
        [rows_of(factor_basis, (lax.axis_index("shard") ^ mask) * block, block) for mask in masks],
        0,
    )
    gate_diff = gate_anchor - gate_local[0]
    partial_factors = lax.dot_general(
        basis, gate_diff, (((1,), (1,)), ((), ())), precision=lax.Precision.HIGHEST
    )
    factor_piece = scatter_factors(partial_factors, bits)
    factor_other = swap(factor_piece)

    parts = []
    cut = local
    for i, (start, size) in enumerate(spans + mixed_spans):
        if i < len(spans):
            part = rows_of(cut, other + start, size)
            if i < window:
                cut = after(local, part)
        else:
            part = mixed[start : start + size]
        if i == len(spans) + len(mixed_spans) - 1:
            part = settled[start - settled_from :]
        ties = [parts[i - window]] if i >= window else []
        if i == gate_before:
            ties += gate
        parts.append(swap(after(part, *ties)))
        if i == 0:
            mixed = (rate / 2) * rows_of(local, own, half) - decay * after(down_moment, parts[0])
            anchor_next = (1 - rate) * after(down_anchor, parts[0]) + (rate / 2) * local
            norm_sent = after(norm_message(norm_local[0], norm_moment), parts[0])
            norm_received = swap(norm_sent)
        if i == len(spans) - 1:
            norm_received = after(norm_received, parts[i])
            settled_from = start
            settled = rows_of(anchor_next, own + start, size)
            settled += (rate / 2) * parts[i] - decay * down_moment[start:]
            factor_piece = (factor_piece + after(factor_other, parts[i])) / groups
            factors = gather_factors(factor_piece, bits)
            gate = advance(gate_anchor, gate_moment, rebuild(factors, basis))
            new_gate_anchor, new_gate_moment = gate
    received, mixed_received = parts[: len(spans)], parts[len(spans) :]
    new_norm_anchor, new_norm_moment = norm_finish(
        norm_anchor, norm_local[0], norm_moment, norm_received
    )

    moment_next = []
    for (start, size), part in zip(spans, received):
        old = down_moment[start : start + size]
        moment_next.append(
            momentum * old
            + rows_of(down_anchor, own + start, size)
            - 0.5 * (rows_of(local, own + start, size) + part)
        )
        value = rows_of(anchor_next, own + start, size) + ((rate / 2) * part - decay * old)
        anchor_next = put_rows(anchor_next, value, own + start)
    for i, ((start, size), part) in enumerate(zip(mixed_spans, mixed_received)):
        if i == pinned:
            anchor_next = add_rows(anchor_next, part, start, half)
        else:
            value = part
            if i < len(mixed_spans) - 1:
                value = value + rows_of(anchor_next, other + start, size)
            anchor_next = put_rows(anchor_next, value, other + start)
    return (
        anchor_next,
        lax.concatenate(moment_next, 0),
        new_norm_anchor,
        new_norm_moment,
        new_gate_anchor,
        new_gate_moment,
    )


def solution(mesh):
    placed = (
        P("shard", "tensor"),
        P("group", "shard", "tensor"),
        P(("shard", "group"), "tensor"),
        P(None, ("shard", "tensor")),
        P("group", None, ("shard", "tensor")),
        P("group", ("shard", "tensor")),
        P("tensor", "shard"),
        P("group", "tensor", "shard"),
        P("tensor", "shard"),
        P(None, "shard"),
    )
    return jax.shard_map(
        body,
        mesh=mesh,
        in_specs=placed,
        out_specs=(
            P("shard", "tensor"),
            P(("shard", "group"), "tensor"),
            P(None, ("shard", "tensor")),
            P("group", ("shard", "tensor")),
            P("tensor", "shard"),
            P("tensor", "shard"),
        ),
        check_vma=False,
    )
```
